128 devices in a mesh: loader: 8 (over z, core), enc: 16 (over x, y).
Axes of the slice: x: 4, y: 4, z: 4, core: 2. Of those that a mesh axis runs over, the one named last changes fastest.
Arguments:
- tiles: bfloat16 [802816, 512], P(('loader', 'enc')), may hold values from -6 to 6
- tile_encoder: int32 [4096], P(('loader', 'enc')), may hold values from -1 to 15, as said below
- tile_slot: int32 [4096], P(('loader', 'enc')), may hold values from -1 to 15, as said below
- slide_counts: int32 [128, 8], P(('loader', 'enc')), may hold values from 0 to 30, as said below
- slide_owner: int32 [1024, 1], P(('loader', 'enc')), may hold values from 0 to 7; in each aligned block of 8 rows (0 to 7, 8 to 15, ...) at most 4 rows name the same one
- w_reduce: bfloat16 [512, 256], replicated, may hold values from -0.25 to 0.25
- b_reduce: float32 [256], replicated, may hold values from -3 to 3
- w_spatial: bfloat16 [2304, 256], replicated, may hold values from -0.125 to 0.125
- b_spatial: float32 [256], replicated, may hold values from -3 to 3
- w_expand: bfloat16 [256, 1024], replicated, may hold values from -0.375 to 0.375
- w_short: bfloat16 [512, 1024], replicated, may hold values from -0.25 to 0.25
- b_join: float32 [1024], replicated, may hold values from -3 to 3
- w_reduce2: bfloat16 [1024, 256], replicated, may hold values from -0.1875 to 0.1875
- b_reduce2: float32 [256], replicated, may hold values from -3 to 3
- w_spatial2: bfloat16 [2304, 256], replicated, may hold values from -0.125 to 0.125
- b_spatial2: float32 [256], replicated, may hold values from -3 to 3
- w_expand2: bfloat16 [256, 1024], replicated, may hold values from -0.375 to 0.375
- b_expand2: float32 [1024], replicated, may hold values from -3 to 3
Outputs:
- slide_features: bfloat16 [4096, 1024], P(('loader', 'enc'))
The draws below stay inside these ranges and needn't reach their ends.
Inputs may be any that keep to these rules, and one draw needn't show every extreme that they name: `tile_encoder`: on each device the tissue tiles are the first tile places, as many as its slides' counts add up to, and only they have an encoder. A device holds at most 30 tissue tiles, and some device holds that many. The encoder lies in the same loader row. Every encoder device gets exactly 16 tissue tiles from the devices of its loader row, and at most 2 from one device; some device sends 2 to one encoder. `tile_slot`: -1 exactly where tile_encoder is -1; the tissue tiles sent to one encoder hold the places 0 to 15 once each. `slide_counts`: A device's counts add up to its number of tissue tiles; slides may hold no tissue tile; some slide holds 30. `slide_owner`: the owner is a loader index in the same enc column. Of the 8 slides of one device at most 4 go to one owner.
All inputs are finite; a program needn't handle non-finite values.
Results may differ from the reference program's by a relative error of at most 0.0034.
Values may be sent and summed in bfloat16 or wider, within the bound.
A program may use at most 128 MiB of HBM per device.

```python
import math
import jax
import jax.numpy as jnp
import numpy as np
from jax import lax

C_IN = 512
C_MID = 256
C_OUT = 1024
GRID = 14
WORK = 16
TPD = 32
CAP = 2
TILES = 4096
SPD = 8
SLIDES = 1024
OCAP = 4
N_LOADER = 8
N_ENC = 16
DEVICES = 128


def layout(key):
    key = jax.random.fold_in(key, 5)
    key_lift, key_perm, key_order, key_prio, key_shift = jax.random.split(key, 5)
    quota = WORK
    lift_size = jax.random.randint(key_lift, (N_LOADER, (N_ENC - 4) // 2), 0, quota - 1)
    fixed_part = jnp.tile(jnp.array([2 * quota - 2, 0, quota + 1, quota + 1], jnp.int32), (N_LOADER, 1))
    tile_loads = jnp.concatenate([fixed_part, quota + lift_size, quota - lift_size], axis=1)
    shuffle = jax.vmap(lambda subkey: jax.random.permutation(subkey, N_ENC))(jax.random.split(key_perm, N_LOADER))
    tile_loads = jnp.take_along_axis(tile_loads, shuffle, axis=1)
    sequence = jax.vmap(lambda subkey: jax.random.permutation(subkey, N_ENC))(jax.random.split(key_order, N_LOADER))
    seq_loads = jnp.take_along_axis(tile_loads, sequence, axis=1)
    seq_start = jnp.cumsum(seq_loads, axis=1) - seq_loads
    inverse = jnp.argsort(sequence, axis=1)
    start_dev = jnp.take_along_axis(seq_start, inverse, axis=1).reshape(-1)
    loads_dev = tile_loads.reshape(-1)
    priority = jax.vmap(lambda subkey: jax.random.permutation(subkey, TPD))(jax.random.split(key_prio, DEVICES))
    positions = jnp.arange(TPD)
    tissue = positions[None, :] < loads_dev[:, None]
    before = tissue[:, None, :] & (priority[:, None, :] < priority[:, :, None])
    standing = jnp.sum(before.astype(jnp.int32), axis=2)
    order_key = start_dev[:, None] + standing
    shifts = jax.random.randint(key_shift, (N_LOADER,), 0, N_ENC)
    shift_dev = jnp.repeat(shifts, N_ENC)
    group_index = order_key // CAP
    encoder = (group_index + shift_dev[:, None]) % N_ENC
    work_slot = group_index // N_ENC * CAP + order_key % CAP
    encoder = jnp.where(tissue, encoder, -1).reshape(-1).astype(jnp.int32)
    work_slot = jnp.where(tissue, work_slot, -1).reshape(-1).astype(jnp.int32)
    return (loads_dev.astype(jnp.int32), encoder, work_slot)


def draw_tile_encoder(key, part):
    return layout(key)[1]


def draw_tile_slot(key, part):
    return layout(key)[2]


def draw_slide_counts(key, part):
    tile_loads = layout(key)[0]
    key = jax.random.fold_in(key, 9)
    cuts = jax.random.randint(key, (DEVICES, SPD - 1), 0, tile_loads[:, None] + 1)
    full_slide = (tile_loads == 2 * WORK - 2) & (jnp.arange(DEVICES) < N_ENC)
    cuts = jnp.where(full_slide[:, None], 0, cuts)
    cuts = jnp.sort(cuts, axis=1)
    edges = jnp.concatenate([jnp.zeros((DEVICES, 1), jnp.int32), cuts.astype(jnp.int32), tile_loads[:, None]], axis=1)
    return (edges[:, 1:] - edges[:, :-1]).astype(jnp.int32)


def block_levels(own_key, shape, cuts, smallest, largest):
    factor_of, own = 1.0, jax.random.fold_in(own_key, 6)
    for position, shards_of in cuts:
        heights = jnp.exp(jax.random.uniform(jax.random.fold_in(own, position), (shards_of,), jnp.float32, smallest / len(cuts), largest / len(cuts)))
        factor_of = factor_of * jnp.repeat(heights, shape[position] // shards_of).reshape([-1 if axis == position else 1 for axis in range(len(shape))])
    return factor_of


def assign_block(rng, own, number, rows, number_of, top, bound, skew):
    ranking = jax.random.permutation(rng, number_of)
    heavy_load, usual = load_shares(number_of, rows * top, bound, skew, True), load_shares(number_of, rows * top, bound, skew, False)
    places = jnp.arange(number_of)

    def named(sizes, turn):
        used = int((sizes > 0).sum())
        fixed = max(1, used // 4)
        passed = fixed + (places - fixed + turn * (used - fixed)) % max(1, number_of - fixed)
        return jnp.zeros((number_of,), jnp.int32).at[ranking[jnp.where(places < fixed, places, passed)]].set(jnp.asarray(sizes, jnp.int32))

    sizes = jnp.where(number % 4 == 0, named(heavy_load, number // 4), named(usual, number - number // 4 - 1))
    mixed = jax.random.permutation(jax.random.fold_in(own, 3), number_of)
    donor, sink = mixed[0:number_of // 2 * 2:2], mixed[1:number_of // 2 * 2:2]
    margin = jnp.minimum(sizes[donor] - 1, bound - sizes[sink]) // 2
    margin = jnp.where((donor == ranking[0]) | (sink == ranking[0]) | (sizes[sink] == 0), 0, jnp.maximum(margin, 0))
    passed = jax.random.randint(jax.random.fold_in(own, 4), (number_of // 2,), 0, 1 << 20) % (margin + 1)
    sizes = sizes.at[donor].add(-passed).at[sink].add(passed)
    members = jnp.searchsorted(jnp.cumsum(sizes), jnp.arange(rows * top), side="right").astype(jnp.int32)
    grid = members.reshape(top, rows).T
    grid = grid[jax.random.permutation(jax.random.fold_in(own, 1), rows)]
    turn = jax.random.randint(jax.random.fold_in(own, 2), (rows, 1), 0, top)
    return jnp.take_along_axis(grid, (jnp.arange(top)[None, :] + turn) % top, axis=1)


def load_shares(number_of, total, bound, slope, full):
    weights = [(1 << 20) // math.isqrt(grade ** slope) + 1 for grade in range(1, number_of + 1)]
    largest = bound if full else min(bound, max(-(-total // number_of), total * weights[0] // sum(weights)))
    least = 1 if total - largest >= number_of - 1 else 0
    holding, rest = [largest] + [least] * (number_of - 1), total - largest - least * (number_of - 1)
    while rest > 0:
        candidates = [i for i in range(1, number_of) if holding[i] < largest] or [i for i in range(1, number_of) if holding[i] < bound]
        pool, left = sum([weights[i] for i in candidates]), rest
        for i in candidates:
            addition = min(bound - holding[i], max(1, left * weights[i] // pool), rest)
            holding[i] = holding[i] + addition
            rest = rest - addition
    return np.array(holding)


def noise(rng, dims, deviation, limit, cuts=(), kind=jnp.bfloat16):
    drawn = jax.random.normal(rng, dims, jnp.float32) * deviation
    if len(cuts) > 0:
        drawn = block_levels(rng, dims, cuts, -0.22, 0.18) * drawn
    return jnp.clip(drawn, min=-limit, max=limit).astype(kind)


def setup_inputs(seed: int = 0) -> dict:
    key_of = jax.random.split(jax.random.key(seed), 19)
    tiles = noise(key_of[0], (TILES * GRID * GRID, C_IN), 1.0, 6.0, ((0, 128),))
    tile_encoder = draw_tile_encoder(jax.random.fold_in(key_of[18], 71), 0)
    tile_slot = draw_tile_slot(jax.random.fold_in(key_of[18], 71), 0)
    slide_counts = draw_slide_counts(jax.random.fold_in(key_of[18], 71), 0)
    slide_owner_keys = jax.random.split(jax.random.fold_in(key_of[4], 1), SLIDES // SPD)
    slide_owner_turns = jax.random.permutation(jax.random.fold_in(key_of[4], 3), SLIDES // SPD)
    slide_owner = jax.vmap(lambda own, number: assign_block(jax.random.fold_in(key_of[4], 2), own, number, SPD, N_LOADER, 1, OCAP, 2))(slide_owner_keys, slide_owner_turns).reshape((SLIDES, 1))
    w_reduce = noise(key_of[5], (C_IN, C_MID), C_IN ** -0.5, 0.25)
    b_reduce = noise(key_of[6], (C_MID,), 0.5, 3.0, (), jnp.float32)
    w_spatial = noise(key_of[7], (9 * C_MID, C_MID), (9 * C_MID) ** -0.5, 0.125)
    b_spatial = noise(key_of[8], (C_MID,), 0.5, 3.0, (), jnp.float32)
    w_expand = noise(key_of[9], (C_MID, C_OUT), C_MID ** -0.5, 0.375)
    w_short = noise(key_of[10], (C_IN, C_OUT), C_IN ** -0.5, 0.25)
    b_join = noise(key_of[11], (C_OUT,), 0.5, 3.0, (), jnp.float32)
    w_reduce2 = noise(key_of[12], (C_OUT, C_MID), C_OUT ** -0.5, 0.1875)
    b_reduce2 = noise(key_of[13], (C_MID,), 0.5, 3.0, (), jnp.float32)
    w_spatial2 = noise(key_of[14], (9 * C_MID, C_MID), (9 * C_MID) ** -0.5, 0.125)
    b_spatial2 = noise(key_of[15], (C_MID,), 0.5, 3.0, (), jnp.float32)
    w_expand2 = noise(key_of[16], (C_MID, C_OUT), C_MID ** -0.5, 0.375)
    b_expand2 = noise(key_of[17], (C_OUT,), 0.5, 3.0, (), jnp.float32)
    return {"tiles": tiles, "tile_encoder": tile_encoder, "tile_slot": tile_slot, "slide_counts": slide_counts, "slide_owner": slide_owner, "w_reduce": w_reduce, "b_reduce": b_reduce, "w_spatial": w_spatial, "b_spatial": b_spatial, "w_expand": w_expand, "w_short": w_short, "b_join": b_join, "w_reduce2": w_reduce2, "b_reduce2": b_reduce2, "w_spatial2": w_spatial2, "b_spatial2": b_spatial2, "w_expand2": w_expand2, "b_expand2": b_expand2}


def spatial_conv(features, weight, bias_row):
    tiles_in, extent, _, channels = features.shape
    padded = jnp.pad(features, ((0, 0), (1, 1), (1, 1), (0, 0)))
    summed = jnp.zeros((tiles_in * extent * extent, weight.shape[1]), jnp.float32) + bias_row
    for tap_index in range(9):
        row_shift = tap_index // 3
        col_shift = tap_index % 3
        window = padded[:, row_shift:row_shift + extent, col_shift:col_shift + extent, :].reshape(-1, channels)
        summed = summed + jnp.dot(window, weight[tap_index * channels:(tap_index + 1) * channels], preferred_element_type=jnp.float32)
    return jax.nn.relu(summed).astype(jnp.bfloat16)


def encode(inputs, w_reduce, b_reduce, w_spatial, b_spatial, w_expand, w_short, b_join, w_reduce2, b_reduce2, w_spatial2, b_spatial2, w_expand2, b_expand2):
    tiles_in, extent, _, channels = inputs.shape
    pixels = inputs.reshape(-1, channels)
    reduced = jax.nn.relu(jnp.dot(pixels, w_reduce, preferred_element_type=jnp.float32) + b_reduce).astype(jnp.bfloat16)
    spatial = spatial_conv(reduced.reshape(tiles_in, extent, extent, -1), w_spatial, b_spatial)
    joined = jax.nn.relu(jnp.dot(spatial, w_expand, preferred_element_type=jnp.float32) + jnp.dot(pixels, w_short, preferred_element_type=jnp.float32) + b_join).astype(jnp.bfloat16)
    narrowed = jax.nn.relu(jnp.dot(joined, w_reduce2, preferred_element_type=jnp.float32) + b_reduce2).astype(jnp.bfloat16)
    spread = spatial_conv(narrowed.reshape(tiles_in, extent, extent, -1), w_spatial2, b_spatial2)
    block_out = jax.nn.relu(jnp.dot(spread, w_expand2, preferred_element_type=jnp.float32) + b_expand2 + joined.astype(jnp.float32))
    return jnp.mean(block_out.reshape(tiles_in, extent * extent, -1), axis=1).astype(jnp.bfloat16)


def reference(tiles, tile_encoder, tile_slot, slide_counts, slide_owner, w_reduce, b_reduce, w_spatial, b_spatial, w_expand, w_short, b_join, w_reduce2, b_reduce2, w_spatial2, b_spatial2, w_expand2, b_expand2):
    weights = (w_reduce, b_reduce, w_spatial, b_spatial, w_expand, w_short, b_join, w_reduce2, b_reduce2, w_spatial2, b_spatial2, w_expand2, b_expand2)
    tile_maps = tiles.reshape(TILES, GRID, GRID, C_IN)
    places = jnp.arange(TILES, dtype=jnp.int32)
    device_of = places // TPD
    row_of = device_of // N_ENC
    tissue = tile_encoder >= 0
    work_place = (row_of * N_ENC + tile_encoder) * WORK + tile_slot
    work_place = jnp.where(tissue, work_place, DEVICES * WORK).astype(jnp.int32)
    source = jnp.zeros((DEVICES * WORK,), jnp.int32).at[work_place].set(places, mode="drop")

    def encode_block(picks):
        return encode(tile_maps[picks], *weights)

    pooled_work = lax.map(encode_block, source.reshape(-1, 4)).reshape(-1, C_OUT)
    pooled = pooled_work[jnp.where(tissue, work_place, 0).astype(jnp.int32)]
    pooled_dev = pooled.reshape(DEVICES, TPD, C_OUT).astype(jnp.float32)
    slide_end = jnp.cumsum(slide_counts, axis=1)
    slide_start = slide_end - slide_counts
    tile_pos = jnp.arange(TPD, dtype=jnp.int32)
    member = ((tile_pos[None, None, :] >= slide_start[:, :, None]) & (tile_pos[None, None, :] < slide_end[:, :, None])).astype(jnp.float32)
    sums = jnp.einsum("dst,dtc->dsc", member, pooled_dev)
    means = (sums / jnp.maximum(slide_counts, 1).astype(jnp.float32)[:, :, None]).astype(jnp.bfloat16)
    owners = slide_owner.reshape(DEVICES, SPD)
    slide_pos = jnp.arange(SPD, dtype=jnp.int32)
    before = (owners[:, None, :] == owners[:, :, None]) & (slide_pos[None, None, :] < slide_pos[None, :, None])
    standing = jnp.sum(before.astype(jnp.int32), axis=2)
    devices_all = jnp.arange(DEVICES, dtype=jnp.int32)
    loader_row = devices_all // N_ENC
    enc_col = devices_all % N_ENC
    target = (owners * N_ENC + enc_col[:, None]) * (N_LOADER * OCAP) + loader_row[:, None] * OCAP + standing
    result = jnp.zeros((DEVICES * N_LOADER * OCAP, C_OUT), jnp.bfloat16)
    return result.at[target.reshape(-1).astype(jnp.int32)].set(means.reshape(-1, C_OUT))
```

```python
import functools

import jax
import jax.numpy as jnp
from jax import lax
from jax.experimental import pallas as pl
from jax.experimental.pallas import tpu as pltpu
from jax.sharding import PartitionSpec as P

GRID = 14
CELLS = GRID * GRID
BATCH = 16
ROWS = BATCH * CELLS
STEP = 2
CHUNK = STEP * GRID * BATCH


def encoder_kernel(
    slide_end,
    slide_count,
    owner,
    b_reduce,
    b_spatial,
    b_join,
    b_reduce2,
    b_spatial2,
    b_expand2,
    tiles,
    w_reduce_hbm,
    w_spatial_hbm,
    w_expand_hbm,
    w_short_hbm,
    w_reduce2_hbm,
    w_spatial2_hbm,
    w_expand2_hbm,
    out,
    w_reduce,
    w_spatial,
    w_join,
    w_reduce2,
    w_spatial2,
    w_expand2,
    arrived,
    spread_out,
    pixels,
    reduced,
    narrowed,
    joined,
    pooled,
    weight_sem,
    tile_sem,
):
    f32, bf16 = jnp.float32, jnp.bfloat16
    slides = slide_count.shape[1]
    tissue = slide_end[0, slides - 1]
    mid = w_expand_hbm.shape[0]
    batches = arrived.shape[0]

    def tile_copy(batch):
        return pltpu.make_async_copy(
            tiles.at[pl.ds(batch * ROWS, ROWS)], arrived.at[batch], tile_sem.at[batch]
        )

    tile_copy(0).start()
    moves = [
        (w_reduce_hbm, w_reduce),
        (w_spatial_hbm, w_spatial),
        (w_expand_hbm, w_join.at[pl.ds(0, mid)]),
        (w_short_hbm, w_join.at[pl.ds(mid, w_short_hbm.shape[0])]),
        (w_reduce2_hbm, w_reduce2),
        (w_spatial2_hbm, w_spatial2),
        (w_expand2_hbm, w_expand2),
    ]
    copies = [
        pltpu.make_async_copy(source, target, weight_sem.at[index])
        for index, (source, target) in enumerate(moves)
    ]
    for copy in copies:
        copy.start()
    for batch in range(1, batches):
        tile_copy(batch).start()

    reduced[...] = jnp.zeros_like(reduced)
    narrowed[...] = jnp.zeros_like(narrowed)
    pooled[...] = jnp.zeros_like(pooled)

    def window(padded, first):
        pieces = [
            padded[pl.ds(first + a, STEP), b : b + GRID, :, :].reshape(CHUNK, mid)
            for a in range(3)
            for b in range(3)
        ]
        return jnp.concatenate(pieces, axis=1)

    def encode(batch):
        def widen(step, _):
            rows = pl.ds(pl.multiple_of(step * CHUNK, CHUNK), CHUNK)
            block = arrived[batch, rows, :].astype(f32)
            for lane in range(4):
                spread_out[lane, rows, :] = block[:, lane * 128 : (lane + 1) * 128]
            return 0

        lax.fori_loop(0, ROWS // CHUNK, widen, 0)

        def turn(row, _):
            for column in range(GRID):
                place = row * GRID + column
                for lane in range(4):
                    piece = spread_out[lane, pl.ds(place, BATCH, stride=CELLS), :]
                    pixels[
                        pl.ds(pl.multiple_of(place * BATCH, BATCH), BATCH),
                        lane * 128 : (lane + 1) * 128,
                    ] = piece.astype(bf16)
            return 0

        lax.fori_loop(0, GRID, turn, 0)

        def first(step, _):
            rows = pl.ds(pl.multiple_of(step * CHUNK, CHUNK), CHUNK)
            value = jnp.dot(pixels[rows, :], w_reduce[...], preferred_element_type=f32)
            value = jnp.maximum(value + b_reduce[...], 0.0).astype(bf16)
            reduced[pl.ds(step * STEP + 1, STEP), 1 : GRID + 1, :, :] = value.reshape(
                STEP, GRID, BATCH, mid
            )
            return 0

        lax.fori_loop(0, GRID // STEP, first, 0)

        def second(step, _):
            rows = pl.ds(pl.multiple_of(step * CHUNK, CHUNK), CHUNK)
            spatial = jnp.dot(
                window(reduced, step * STEP), w_spatial[...], preferred_element_type=f32
            )
            spatial = jnp.maximum(spatial + b_spatial[...], 0.0).astype(bf16)
            both = jnp.concatenate([spatial, pixels[rows, :]], axis=1)
            value = jnp.dot(both, w_join[...], preferred_element_type=f32)
            value = jnp.maximum(value + b_join[...], 0.0).astype(bf16)
            joined[rows, :] = value
            value = jnp.dot(value, w_reduce2[...], preferred_element_type=f32)
            value = jnp.maximum(value + b_reduce2[...], 0.0).astype(bf16)
            narrowed[pl.ds(step * STEP + 1, STEP), 1 : GRID + 1, :, :] = value.reshape(
                STEP, GRID, BATCH, mid
            )
            return 0

        lax.fori_loop(0, GRID // STEP, second, 0)

        def third(step, total):
            rows = pl.ds(pl.multiple_of(step * CHUNK, CHUNK), CHUNK)
            spread = jnp.dot(
                window(narrowed, step * STEP), w_spatial2[...], preferred_element_type=f32
            )
            spread = jnp.maximum(spread + b_spatial2[...], 0.0).astype(bf16)
            value = jnp.dot(spread, w_expand2[...], preferred_element_type=f32)
            value = jnp.maximum(value + b_expand2[...] + joined[rows, :].astype(f32), 0.0)
            return total + jnp.sum(value.reshape(STEP * GRID, BATCH, -1), axis=0)

        total = lax.fori_loop(
            0, GRID // STEP, third, jnp.zeros((BATCH, joined.shape[1]), f32)
        )
        pooled[batch * BATCH : (batch + 1) * BATCH, :] = (total / CELLS).astype(bf16)

    for batch in range(batches):
        tile_copy(batch).wait()
        if batch == 0:
            for copy in copies:
                copy.wait()
        pl.when(tissue > batch * BATCH)(functools.partial(encode, batch))

    received = out.shape[0]
    shape = (received, pooled.shape[0])
    row = lax.broadcasted_iota(jnp.int32, shape, 0)
    place = lax.broadcasted_iota(jnp.int32, shape, 1)
    row_only = lax.broadcasted_iota(jnp.int32, (received, 1), 0)
    chosen = jnp.zeros(shape, f32)
    divisor = jnp.ones((received, 1), f32)
    cap = received // 8
    for j in range(slides):
        standing = jnp.int32(0)
        for earlier in range(j):
            standing += (owner[earlier, 0] == owner[j, 0]).astype(jnp.int32)
        target = owner[j, 0] * cap + standing
        end, count = slide_end[0, j], slide_count[0, j]
        member = (row == target) & (place >= end - count) & (place < end)
        chosen = jnp.where(member, 1.0, chosen)
        size = jnp.maximum(count, 1).astype(f32)
        divisor = jnp.where(row_only == target, size, divisor)
    sums = jnp.dot(chosen.astype(bf16), pooled[...], preferred_element_type=f32)
    out[...] = (sums / divisor).astype(bf16)


def body(
    tiles,
    tile_encoder,
    tile_slot,
    slide_counts,
    slide_owner,
    w_reduce,
    b_reduce,
    w_spatial,
    b_spatial,
    w_expand,
    w_short,
    b_join,
    w_reduce2,
    b_reduce2,
    w_spatial2,
    b_spatial2,
    w_expand2,
    b_expand2,
):
    bf16, f32 = jnp.bfloat16, jnp.float32
    places = tile_encoder.shape[0]
    loaders = lax.axis_size("loader")
    c_in, c_mid = w_reduce.shape
    c_out = w_expand.shape[1]
    batches = places // BATCH
    slide_end = jnp.cumsum(slide_counts, axis=1)
    smem = pl.BlockSpec(memory_space=pltpu.SMEM)
    vmem = pl.BlockSpec(memory_space=pltpu.VMEM)
    anywhere = pl.BlockSpec(memory_space=pl.ANY)
    packed = pl.pallas_call(
        encoder_kernel,
        out_shape=jax.ShapeDtypeStruct((places, c_out), bf16),
        in_specs=[smem] * 3 + [vmem] * 6 + [anywhere] * 8,
        out_specs=vmem,
        scratch_shapes=[
            pltpu.VMEM(w_reduce.shape, bf16),
            pltpu.VMEM(w_spatial.shape, bf16),
            pltpu.VMEM((c_mid + c_in, c_out), bf16),
            pltpu.VMEM(w_reduce2.shape, bf16),
            pltpu.VMEM(w_spatial2.shape, bf16),
            pltpu.VMEM(w_expand2.shape, bf16),
            pltpu.VMEM((batches, ROWS, c_in), bf16),
            pltpu.VMEM((4, ROWS, 128), f32),
            pltpu.VMEM((ROWS, c_in), bf16),
            pltpu.VMEM((GRID + 2, GRID + 2, BATCH, c_mid), bf16),
            pltpu.VMEM((GRID + 2, GRID + 2, BATCH, c_mid), bf16),
            pltpu.VMEM((ROWS, c_out), bf16),
            pltpu.VMEM((places, c_out), bf16),
            pltpu.SemaphoreType.DMA((7,)),
            pltpu.SemaphoreType.DMA((batches,)),
        ],
        compiler_params=pltpu.CompilerParams(vmem_limit_bytes=60 * 1024 * 1024),
        name="encode_tiles",
    )(
        slide_end,
        slide_counts,
        slide_owner,
        b_reduce[None],
        b_spatial[None],
        b_join[None],
        b_reduce2[None],
        b_spatial2[None],
        b_expand2[None],
        tiles,
        w_reduce,
        w_spatial,
        w_expand,
        w_short,
        w_reduce2,
        w_spatial2,
        w_expand2,
    )
    delivered = lax.all_to_all(
        packed.reshape(loaders, places // loaders, -1),
        "loader",
        split_axis=0,
        concat_axis=0,
        tiled=True,
    )
    return delivered.reshape(places, -1)


def solution(mesh):
    split = P(("loader", "enc"))
    placed = (split,) * 5 + (P(),) * 13
    return jax.shard_map(
        body, mesh=mesh, in_specs=placed, out_specs=split, check_vma=False
    )
```

```python
import functools

import jax
import jax.numpy as jnp
from jax import lax
from jax.experimental import pallas as pl
from jax.experimental.pallas import tpu as pltpu
from jax.sharding import PartitionSpec as P

MESH = pl.DeviceIdType.MESH
GRID = 14
CELLS = GRID * GRID
BATCH = 8
ROWS = BATCH * CELLS
LINE = GRID * BATCH
PAIRS = GRID // 2 + 1


def encoder_kernel(
    counts_ref,
    owner_ref,
    b_reduce,
    b_spatial,
    b_join,
    b_reduce2,
    b_spatial2,
    b_expand2,
    tiles,
    w_reduce_hbm,
    w_spatial_hbm,
    w_expand_hbm,
    w_short_hbm,
    w_reduce2_hbm,
    w_spatial2_hbm,
    w_expand2_hbm,
    out,
    w_reduce,
    w_spatial,
    w_join,
    w_reduce2,
    w_spatial2,
    w_expand2,
    arrived,
    widened,
    pixels,
    reduced_even,
    reduced_odd,
    narrowed_even,
    narrowed_odd,
    spatial,
    joined,
    residual,
    pooled,
    weight_sem,
    tile_sem,
):
    f32, bf16 = jnp.float32, jnp.bfloat16
    slides = counts_ref.shape[1]
    mid = w_expand_hbm.shape[0]
    most = arrived.shape[0]
    counts = [counts_ref[0, j] for j in range(slides)]
    ends = [counts[0]]
    for count in counts[1:]:
        ends.append(ends[-1] + count)
    batches = (ends[-1] + BATCH - 1) // BATCH

    def tile_copy(batch):
        rows = pl.ds(pl.multiple_of(batch * ROWS, ROWS), ROWS)
        return pltpu.make_async_copy(tiles.at[rows], arrived.at[batch], tile_sem.at[batch])

    moves = [
        (w_reduce_hbm, w_reduce),
        (w_spatial_hbm, w_spatial),
        (w_expand_hbm, w_join.at[pl.ds(0, mid)]),
        (w_short_hbm, w_join.at[pl.ds(mid, w_short_hbm.shape[0])]),
        (w_reduce2_hbm, w_reduce2),
        (w_spatial2_hbm, w_spatial2),
        (w_expand2_hbm, w_expand2),
    ]
    copies = [
        pltpu.make_async_copy(source, target, weight_sem.at[index])
        for index, (source, target) in enumerate(moves)
    ]
    pl.when(batches > 0)(lambda: tile_copy(0).start())
    for copy in copies:
        copy.start()
    for batch in range(1, most):
        pl.when(batches > batch)(functools.partial(lambda b: tile_copy(b).start(), batch))

    border = jnp.zeros((1,) + reduced_even.shape[1:], bf16)
    for padded in (reduced_even, reduced_odd, narrowed_even, narrowed_odd):
        padded[0:1] = border
        padded[GRID + 1 : GRID + 2] = border
    pooled[...] = jnp.zeros_like(pooled)

    half = GRID // 2
    order = [(lane, k) for k in range(half) for lane in range(2)]

    def image_row(mxu, k):
        return k if mxu == 0 else GRID - 1 - k

    def keep(even, odd, bias):
        def finish(i, n, value):
            value = jnp.maximum(value + bias[...], 0.0).reshape(GRID, BATCH, mid)
            side = jnp.zeros((1, BATCH, mid), f32)
            whole = jnp.concatenate([side, value, side], axis=0)
            even[i + 1] = whole.reshape(PAIRS, 2 * BATCH, mid).astype(bf16)
            odd[i + 1, 0 : PAIRS - 1] = value.reshape(
                PAIRS - 1, 2 * BATCH, mid
            ).astype(bf16)

        return finish

    def tap(even, odd):
        def left(i, k):
            a, b = k // 3, k % 3
            source = odd if b == 1 else even
            first = 1 if b == 2 else 0
            piece = source[i + a, first : first + PAIRS - 1]
            return piece.reshape(LINE, mid)

        return left

    def line(i):
        return slice(i * LINE, (i + 1) * LINE)

    def lanes(n):
        return slice(n * mid, (n + 1) * mid)

    def plain(target, bias):
        def finish(i, n, value):
            value = jnp.maximum(value + bias[:, lanes(n)], 0.0).astype(bf16)
            target[line(i), lanes(n)] = value

        return finish

    def join(i, n, value):
        value = jnp.maximum(value + b_join[:, lanes(n)], 0.0)
        joined[line(i), lanes(n)] = value.astype(bf16)
        residual[line(i), lanes(n)] = value + b_expand2[:, lanes(n)]

    def tiles_of(ref):
        return lambda i, k: ref[line(i), lanes(k)]

    def run(stages, *accs):
        passes = []
        for left, weights, finish, lag, beside in stages:
            depth, width = weights.shape[0] // mid, weights.shape[1] // mid
            for n in range(width):
                for k in range(depth):
                    ahead = lag if n == 0 else 0
                    passes.append((left, weights, finish, n, k, k == depth - 1, ahead, beside))

        def push(index):
            _, weights, _, n, k, _, _, _ = passes[index]
            for mxu in range(2):
                pltpu.matmul_push_rhs(
                    weights[lanes(k), lanes(n)], staging_register=index % 2, mxu_index=mxu
                )

        def pop(finish, n, k):
            for mxu in range(2):
                finish(image_row(mxu, k), n, pltpu.matmul_pop(accs[mxu * half + k]))

        push(0)
        waiting = None
        for index, (left, weights, finish, n, k, last, lag, beside) in enumerate(passes):
            if index + 1 < len(passes):
                push(index + 1)
            popped = 0
            for block in range(half):
                if beside is not None:
                    beside(k * half + block)
                if waiting is not None:
                    while popped < min(half, block + 1 + lag):
                        pop(*waiting, popped)
                        popped += 1
                for mxu in range(2):
                    pltpu.matmul_acc_lhs(
                        accs[mxu * half + block],
                        left(image_row(mxu, block), k),
                        load_staged_rhs=index % 2 if block == 0 else None,
                    )
            waiting = (finish, n) if last else None
        for block in range(half):
            pop(*waiting, block)

    def widen(batch, i):
        block = arrived[batch, line(i), :].astype(f32)
        for lane in range(4):
            widened[lane, line(i), :] = block[:, lane * 128 : (lane + 1) * 128]

    def turn(pair):
        for lane in range(4):
            two = [
                widened[lane, pl.ds(2 * pair + k, BATCH, stride=CELLS), :] for k in range(2)
            ]
            pixels[
                pair * 2 * BATCH : (pair + 1) * 2 * BATCH, lane * 128 : (lane + 1) * 128
            ] = jnp.concatenate(two, axis=0).astype(bf16)

    @pl.when(batches > 0)
    def _():
        tile_copy(0).wait()
        for i in range(GRID):
            widen(0, i)
        for pair in range(CELLS // 2):
            turn(pair)

    for copy in copies:
        copy.wait()

    def encode(batch, _):
        pl.when(batch + 1 < batches)(lambda: tile_copy(batch + 1).wait())
        following = jnp.minimum(batch + 1, most - 1)
        totals = {}

        def widen_next(step):
            if step % 4 == 0 and step // 4 < GRID:
                widen(following, step // 4)

        def turn_next(step):
            for pair in (2 * step, 2 * step + 1):
                if pair < CELLS // 2:
                    turn(pair)

        def pool(i, n, value):
            value = jnp.maximum(value + residual[line(i), lanes(n)], 0.0)
            value = value.reshape(GRID, BATCH, mid)
            value = jnp.sum(value, axis=0)
            totals[n] = totals[n] + value if n in totals else value

        def both(i, k):
            if k == 0:
                return spatial[line(i), :]
            return pixels[line(i), lanes(k - 1)]

        stages = [
            (tiles_of(pixels), w_reduce, keep(reduced_even, reduced_odd, b_reduce), 0, None),
            (tap(reduced_even, reduced_odd), w_spatial, plain(spatial, b_spatial), 1, widen_next),
            (both, w_join, join, 1, None),
            (tiles_of(joined), w_reduce2, keep(narrowed_even, narrowed_odd, b_reduce2), 1, None),
            (tap(narrowed_even, narrowed_odd), w_spatial2, plain(spatial, b_spatial2), 1, turn_next),
            (tiles_of(spatial), w_expand2, pool, 1, None),
        ]
        accumulators = [
            pltpu.ACC(mxu)((LINE, mid), f32) for mxu in range(2) for _ in range(half)
        ]

        def whole(*accs):
            run(stages, *accs)
            rows = pl.ds(pl.multiple_of(batch * BATCH, BATCH), BATCH)
            for n, total in totals.items():
                pooled[rows, lanes(n)] = total / CELLS

        pl.run_scoped(whole, *accumulators)
        return 0

    lax.fori_loop(0, batches, encode, 0)

    rows = out.shape[0]
    width = pooled.shape[1] // mid
    cap = rows // (8 * width)
    row = lax.broadcasted_iota(jnp.int32, (rows, mid), 0)
    place = lax.broadcasted_iota(jnp.int32, (rows, mid), 1)
    column = lax.broadcasted_iota(jnp.int32, (rows, 1), 0)
    divisor = jnp.ones((rows, 1), f32)
    owners = [owner_ref[0, j] for j in range(slides)]
    chosen = jnp.zeros((rows, mid), f32)
    slot = row // (width * cap) * cap + row % cap
    slot_column = column // (width * cap) * cap + column % cap
    for j in range(slides):
        standing = jnp.int32(0)
        for earlier in range(j):
            standing += (owners[earlier] == owners[j]).astype(jnp.int32)
        target = owners[j] * cap + standing
        member = (slot == target) & (place >= ends[j] - counts[j]) & (place < ends[j])
        chosen = jnp.where(member, 1.0, chosen)
        size = jnp.maximum(counts[j], 1).astype(f32)
        divisor = jnp.where(slot_column == target, size, divisor)

    def average(acc):
        for n in range(width):
            pltpu.matmul_push_rhs(
                pooled[:, lanes(n)].astype(bf16), staging_register=n % 2, mxu_index=0
            )
            here = jnp.where(row // cap % width == n, chosen, 0.0).astype(bf16)
            pltpu.matmul_acc_lhs(acc, here, load_staged_rhs=n % 2)
        out[...] = (pltpu.matmul_pop(acc) / divisor).astype(bf16)

    pl.run_scoped(average, pltpu.ACC(0)((rows, mid), f32))


def deliver_kernel(packed, out, received, send_sem, receive_sem):
    bf16, f32 = jnp.bfloat16, jnp.float32
    loaders = lax.axis_size("loader")
    me = lax.axis_index("loader")
    size = packed.shape[0] // loaders

    def block(index):
        return pl.ds(pl.multiple_of(index * size, size), size)

    barrier = pltpu.get_barrier_semaphore()
    peers = [lax.rem(me + step, loaders) for step in range(1, loaders)]
    for peer in peers:
        pl.semaphore_signal(barrier, inc=1, device_id={"loader": peer}, device_id_type=MESH)
    pl.semaphore_wait(barrier, loaders - 1)
    copies = [
        pltpu.make_async_remote_copy(
            src_ref=packed.at[block(peer)],
            dst_ref=received.at[block(me)],
            send_sem=send_sem.at[index],
            recv_sem=receive_sem.at[index],
            device_id={"loader": peer},
            device_id_type=MESH,
        )
        for index, peer in enumerate(peers)
    ]
    for copy in copies:
        copy.start()
    received[block(me), :] = packed[block(me), :]
    for copy in copies:
        copy.wait()

    rows, lanes = out.shape[0], packed.shape[1]
    width = out.shape[1] // lanes
    cap = rows // loaders
    shape = (rows, packed.shape[0])
    row = lax.broadcasted_iota(jnp.int32, shape, 0)
    column = lax.broadcasted_iota(jnp.int32, shape, 1)
    for n in range(width):
        source = (row // cap * width + n) * cap + row % cap
        chosen = (column == source).astype(f32).astype(bf16)
        value = jnp.dot(chosen, received[...], preferred_element_type=f32)
        out[:, n * lanes : (n + 1) * lanes] = value.astype(bf16)


def encode_local(
    tiles,
    slide_counts,
    slide_owner,
    w_reduce,
    b_reduce,
    w_spatial,
    b_spatial,
    w_expand,
    w_short,
    b_join,
    w_reduce2,
    b_reduce2,
    w_spatial2,
    b_spatial2,
    w_expand2,
    b_expand2,
    loaders,
):
    bf16, f32 = jnp.bfloat16, jnp.float32
    places = tiles.shape[0] // CELLS
    c_in, c_mid = w_reduce.shape
    c_out = w_expand.shape[1]
    cap = places // loaders
    batches = places // BATCH
    smem = pl.BlockSpec(memory_space=pltpu.SMEM)
    vmem = pl.BlockSpec(memory_space=pltpu.VMEM)
    anywhere = pl.BlockSpec(memory_space=pl.ANY)
    bordered = (GRID + 2, PAIRS, 2 * BATCH, c_mid)
    return pl.pallas_call(
        encoder_kernel,
        out_shape=jax.ShapeDtypeStruct((loaders * (c_out // c_mid) * cap, c_mid), bf16),
        in_specs=[smem] * 2 + [vmem] * 6 + [anywhere] * 8,
        out_specs=vmem,
        scratch_shapes=[
            pltpu.VMEM(w_reduce.shape, bf16),
            pltpu.VMEM(w_spatial.shape, bf16),
            pltpu.VMEM((c_mid + c_in, c_out), bf16),
            pltpu.VMEM(w_reduce2.shape, bf16),
            pltpu.VMEM(w_spatial2.shape, bf16),
            pltpu.VMEM(w_expand2.shape, bf16),
            pltpu.VMEM((batches, ROWS, c_in), bf16),
            pltpu.VMEM((4, ROWS, 128), f32),
            pltpu.VMEM((ROWS, c_in), bf16),
            pltpu.VMEM(bordered, bf16),
            pltpu.VMEM(bordered, bf16),
            pltpu.VMEM(bordered, bf16),
            pltpu.VMEM(bordered, bf16),
            pltpu.VMEM((ROWS, c_mid), bf16),
            pltpu.VMEM((ROWS, c_out), bf16),
            pltpu.VMEM((ROWS, c_out), f32),
            pltpu.VMEM((c_mid, c_out), f32),
            pltpu.SemaphoreType.DMA((7,)),
            pltpu.SemaphoreType.DMA((batches,)),
        ],
        compiler_params=pltpu.CompilerParams(vmem_limit_bytes=60 * 1024 * 1024),
        name="encode_tiles",
    )(
        slide_counts,
        slide_owner.T,
        b_reduce[None],
        b_spatial[None],
        b_join[None],
        b_reduce2[None],
        b_spatial2[None],
        b_expand2[None],
        tiles,
        w_reduce,
        w_spatial,
        w_expand,
        w_short,
        w_reduce2,
        w_spatial2,
        w_expand2,
    )


def deliver(packed, places, c_out):
    vmem = pl.BlockSpec(memory_space=pltpu.VMEM)
    others = lax.axis_size("loader") - 1
    return pl.pallas_call(
        deliver_kernel,
        out_shape=jax.ShapeDtypeStruct((places, c_out), packed.dtype),
        in_specs=[vmem],
        out_specs=vmem,
        scratch_shapes=[
            pltpu.VMEM(packed.shape, packed.dtype),
            pltpu.SemaphoreType.DMA((others,)),
            pltpu.SemaphoreType.DMA((others,)),
        ],
        compiler_params=pltpu.CompilerParams(collective_id=0, has_side_effects=True),
        name="deliver_slides",
    )(packed)


def body(tiles, tile_encoder, tile_slot, slide_counts, slide_owner, *weights):
    packed = encode_local(
        tiles, slide_counts, slide_owner, *weights, loaders=lax.axis_size("loader")
    )
    return deliver(packed, tile_encoder.shape[0], weights[4].shape[1])


def solution(mesh):
    split = P(("loader", "enc"))
    placed = (split,) * 5 + (P(),) * 13
    return jax.shard_map(
        body, mesh=mesh, in_specs=placed, out_specs=split, check_vma=False
    )
```

```python
import functools

import jax
import jax.numpy as jnp
from jax import lax
from jax.experimental import pallas as pl
from jax.experimental.pallas import tpu as pltpu
from jax.sharding import PartitionSpec as P

MESH = pl.DeviceIdType.MESH
GRID = 14
CELLS = GRID * GRID
BATCH = 8
ROWS = BATCH * CELLS
LINE = GRID * BATCH
PAIRS = GRID // 2 + 1


def encoder_kernel(
    counts_ref,
    owner_ref,
    b_reduce,
    b_spatial,
    b_join,
    b_reduce2,
    b_spatial2,
    b_expand2,
    tiles,
    w_reduce_hbm,
    w_spatial_hbm,
    w_expand_hbm,
    w_short_hbm,
    w_reduce2_hbm,
    w_spatial2_hbm,
    w_expand2_hbm,
    out,
    w_reduce,
    w_spatial,
    w_join,
    w_reduce2,
    w_spatial2,
    w_expand2,
    arrived,
    widened,
    pixels,
    reduced_even,
    reduced_odd,
    narrowed_even,
    narrowed_odd,
    spatial,
    joined,
    residual,
    pooled,
    packed,
    received,
    weight_sem,
    tile_sem,
    send_sem,
    receive_sem,
):
    f32, bf16 = jnp.float32, jnp.bfloat16
    slides = counts_ref.shape[1]
    mid = w_expand_hbm.shape[0]
    most = arrived.shape[0]
    counts = [counts_ref[0, j] for j in range(slides)]
    ends = [counts[0]]
    for count in counts[1:]:
        ends.append(ends[-1] + count)

    loaders = lax.axis_size("loader")
    me = lax.axis_index("loader")
    peers = [lax.rem(me + step, loaders) for step in range(1, loaders)]
    barrier = pltpu.get_barrier_semaphore()
    for peer in peers:
        pl.semaphore_signal(barrier, inc=1, device_id={"loader": peer}, device_id_type=MESH)

    def tile_copy(batch):
        rows = pl.ds(pl.multiple_of(batch * ROWS, ROWS), ROWS)
        return pltpu.make_async_copy(tiles.at[rows], arrived.at[batch], tile_sem.at[batch])

    moves = [
        (w_reduce_hbm, w_reduce),
        (w_spatial_hbm, w_spatial),
        (w_expand_hbm, w_join.at[pl.ds(0, mid)]),
        (w_short_hbm, w_join.at[pl.ds(mid, w_short_hbm.shape[0])]),
        (w_reduce2_hbm, w_reduce2),
        (w_spatial2_hbm, w_spatial2),
        (w_expand2_hbm, w_expand2),
    ]
    copies = [
        pltpu.make_async_copy(source, target, weight_sem.at[index])
        for index, (source, target) in enumerate(moves)
    ]
    tile_copy(0).start()
    for copy in copies:
        copy.start()
    for batch in range(1, most):
        tile_copy(batch).start()

    border = jnp.zeros((1,) + reduced_even.shape[1:], bf16)
    for padded in (reduced_even, reduced_odd, narrowed_even, narrowed_odd):
        padded[0:1] = border
        padded[GRID + 1 : GRID + 2] = border
    pooled[...] = jnp.zeros_like(pooled)
    received[packed.shape[0] :, :] = jnp.zeros((mid - packed.shape[0], mid), bf16)

    half = GRID // 2
    order = [(lane, k) for k in range(half) for lane in range(2)]

    def image_row(mxu, k):
        return k if mxu == 0 else GRID - 1 - k

    def keep(even, odd, bias):
        def finish(i, n, value):
            value = jnp.maximum(value + bias[...], 0.0).reshape(GRID, BATCH, mid)
            side = jnp.zeros((1, BATCH, mid), f32)
            whole = jnp.concatenate([side, value, side], axis=0)
            even[i + 1] = whole.reshape(PAIRS, 2 * BATCH, mid).astype(bf16)
            odd[i + 1, 0 : PAIRS - 1] = value.reshape(
                PAIRS - 1, 2 * BATCH, mid
            ).astype(bf16)

        return finish

    def tap(even, odd):
        def left(i, k):
            a, b = k // 3, k % 3
            source = odd if b == 1 else even
            first = 1 if b == 2 else 0
            piece = source[i + a, first : first + PAIRS - 1]
            return piece.reshape(LINE, mid)

        return left

    def line(i):
        return slice(i * LINE, (i + 1) * LINE)

    def lanes(n):
        return slice(n * mid, (n + 1) * mid)

    def plain(target, bias):
        def finish(i, n, value):
            value = jnp.maximum(value + bias[:, lanes(n)], 0.0).astype(bf16)
            target[line(i), lanes(n)] = value

        return finish

    def join(i, n, value):
        value = jnp.maximum(value + b_join[:, lanes(n)], 0.0)
        joined[line(i), lanes(n)] = value.astype(bf16)
        residual[line(i), lanes(n)] = value + b_expand2[:, lanes(n)]

    def tiles_of(ref):
        return lambda i, k: ref[line(i), lanes(k)]

    def run(stages, *accs):
        passes = []
        for left, weights, finish, lag, beside in stages:
            depth, width = weights.shape[0] // mid, weights.shape[1] // mid
            for n in range(width):
                for k in range(depth):
                    ahead = lag if n == 0 else 0
                    passes.append((left, weights, finish, n, k, k == depth - 1, ahead, beside))

        def push(index):
            _, weights, _, n, k, _, _, _ = passes[index]
            for mxu in range(2):
                pltpu.matmul_push_rhs(
                    weights[lanes(k), lanes(n)], staging_register=index % 2, mxu_index=mxu
                )

        def pop(finish, n, k):
            for mxu in range(2):
                finish(image_row(mxu, k), n, pltpu.matmul_pop(accs[mxu * half + k]))

        push(0)
        waiting = None
        for index, (left, weights, finish, n, k, last, lag, beside) in enumerate(passes):
            if index + 1 < len(passes):
                push(index + 1)
            popped = 0
            for block in range(half):
                if beside is not None:
                    beside(k * half + block)
                if waiting is not None:
                    while popped < min(half, block + 1 + lag):
                        pop(*waiting, popped)
                        popped += 1
                for mxu in range(2):
                    pltpu.matmul_acc_lhs(
                        accs[mxu * half + block],
                        left(image_row(mxu, block), k),
                        load_staged_rhs=index % 2 if block == 0 else None,
                    )
            waiting = (finish, n) if last else None
        for block in range(half):
            pop(*waiting, block)

    def widen(batch, i):
        block = arrived[batch, line(i), :].astype(f32)
        for lane in range(4):
            widened[lane, line(i), :] = block[:, lane * 128 : (lane + 1) * 128]

    def turn(pair):
        for lane in range(4):
            two = [
                widened[lane, pl.ds(2 * pair + k, BATCH, stride=CELLS), :] for k in range(2)
            ]
            pixels[
                pair * 2 * BATCH : (pair + 1) * 2 * BATCH, lane * 128 : (lane + 1) * 128
            ] = jnp.concatenate(two, axis=0).astype(bf16)

    tile_copy(0).wait()
    for i in range(GRID):
        widen(0, i)
    for pair in range(CELLS // 2):
        turn(pair)

    for copy in copies:
        copy.wait()

    def encode(batch, _):
        pl.when(batch + 1 < most)(lambda: tile_copy(batch + 1).wait())
        following = lax.rem(batch + 1, most)
        totals = {}

        def widen_next(step):
            if step % 4 == 0 and step // 4 < GRID:
                widen(following, step // 4)

        def turn_next(step):
            for pair in (2 * step, 2 * step + 1):
                if pair < CELLS // 2:
                    turn(pair)

        def pool(i, n, value):
            value = jnp.maximum(value + residual[line(i), lanes(n)], 0.0)
            value = value.reshape(GRID, BATCH, mid)
            value = jnp.sum(value, axis=0)
            totals[n] = totals[n] + value if n in totals else value

        def both(i, k):
            if k == 0:
                return spatial[line(i), :]
            return pixels[line(i), lanes(k - 1)]

        stages = [
            (tiles_of(pixels), w_reduce, keep(reduced_even, reduced_odd, b_reduce), 0, None),
            (tap(reduced_even, reduced_odd), w_spatial, plain(spatial, b_spatial), 1, widen_next),
            (both, w_join, join, 1, None),
            (tiles_of(joined), w_reduce2, keep(narrowed_even, narrowed_odd, b_reduce2), 1, None),
            (tap(narrowed_even, narrowed_odd), w_spatial2, plain(spatial, b_spatial2), 1, turn_next),
            (tiles_of(spatial), w_expand2, pool, 1, None),
        ]
        accumulators = [
            pltpu.ACC(mxu)((LINE, mid), f32) for mxu in range(2) for _ in range(half)
        ]

        def whole(*accs):
            run(stages, *accs)
            rows = pl.ds(pl.multiple_of(batch * BATCH, BATCH), BATCH)
            for n, total in totals.items():
                pooled[rows, lanes(n)] = total / CELLS

        pl.run_scoped(whole, *accumulators)
        return 0

    lax.fori_loop(0, most, encode, 0)

    rows = packed.shape[0]
    width = pooled.shape[1] // mid
    cap = rows // (loaders * width)
    row = lax.broadcasted_iota(jnp.int32, (rows, mid), 0)
    place = lax.broadcasted_iota(jnp.int32, (rows, mid), 1)
    column = lax.broadcasted_iota(jnp.int32, (rows, 1), 0)
    divisor = jnp.ones((rows, 1), f32)
    owners = [owner_ref[0, j] for j in range(slides)]
    chosen = jnp.zeros((rows, mid), f32)
    slot = row // (width * cap) * cap + row % cap
    slot_column = column // (width * cap) * cap + column % cap
    for j in range(slides):
        standing = jnp.int32(0)
        for earlier in range(j):
            standing += (owners[earlier] == owners[j]).astype(jnp.int32)
        target = owners[j] * cap + standing
        member = (slot == target) & (place >= ends[j] - counts[j]) & (place < ends[j])
        chosen = jnp.where(member, 1.0, chosen)
        size = jnp.maximum(counts[j], 1).astype(f32)
        divisor = jnp.where(slot_column == target, size, divisor)

    def average(acc):
        for n in range(width):
            pltpu.matmul_push_rhs(
                pooled[:, lanes(n)].astype(bf16), staging_register=n % 2, mxu_index=0
            )
            here = jnp.where(row // cap % width == n, chosen, 0.0).astype(bf16)
            pltpu.matmul_acc_lhs(acc, here, load_staged_rhs=n % 2)
        packed[...] = (pltpu.matmul_pop(acc) / divisor).astype(bf16)

    pl.run_scoped(average, pltpu.ACC(0)((rows, mid), f32))

    size = width * cap

    def block(index):
        return pl.ds(pl.multiple_of(index * size, size), size)

    pl.semaphore_wait(barrier, loaders - 1)
    sends = [
        pltpu.make_async_remote_copy(
            src_ref=packed.at[block(peer)],
            dst_ref=received.at[block(me)],
            send_sem=send_sem.at[index],
            recv_sem=receive_sem.at[index],
            device_id={"loader": peer},
            device_id_type=MESH,
        )
        for index, peer in enumerate(peers)
    ]
    for send in sends:
        send.start()
    received[block(me), :] = packed[block(me), :]

    shape = (out.shape[0], mid)
    row = lax.broadcasted_iota(jnp.int32, shape, 0)
    column = lax.broadcasted_iota(jnp.int32, shape, 1)

    def unpack(*accs):
        pltpu.matmul_push_rhs(received[...], staging_register=0, mxu_index=0)
        for n, acc in enumerate(accs):
            source = (row // cap * width + n) * cap + row % cap
            here = jnp.where(column == source, 1.0, 0.0).astype(bf16)
            pltpu.matmul_acc_lhs(acc, here, load_staged_rhs=0 if n == 0 else None)
        for n, acc in enumerate(accs):
            out[:, lanes(n)] = pltpu.matmul_pop(acc).astype(bf16)

    for send in sends:
        send.wait()
    pl.run_scoped(unpack, *[pltpu.ACC(0)(shape, f32) for _ in range(width)])


def encode_local(
    tiles,
    slide_counts,
    slide_owner,
    w_reduce,
    b_reduce,
    w_spatial,
    b_spatial,
    w_expand,
    w_short,
    b_join,
    w_reduce2,
    b_reduce2,
    w_spatial2,
    b_spatial2,
    w_expand2,
    b_expand2,
):
    bf16, f32 = jnp.bfloat16, jnp.float32
    places = tiles.shape[0] // CELLS
    c_in, c_mid = w_reduce.shape
    c_out = w_expand.shape[1]
    loaders = lax.axis_size("loader")
    packed_rows = places * (c_out // c_mid)
    batches = places // BATCH
    smem = pl.BlockSpec(memory_space=pltpu.SMEM)
    vmem = pl.BlockSpec(memory_space=pltpu.VMEM)
    anywhere = pl.BlockSpec(memory_space=pl.ANY)
    bordered = (GRID + 2, PAIRS, 2 * BATCH, c_mid)
    return pl.pallas_call(
        encoder_kernel,
        out_shape=jax.ShapeDtypeStruct((places, c_out), bf16),
        in_specs=[smem] * 2 + [vmem] * 6 + [anywhere] * 8,
        out_specs=vmem,
        scratch_shapes=[
            pltpu.VMEM(w_reduce.shape, bf16),
            pltpu.VMEM(w_spatial.shape, bf16),
            pltpu.VMEM((c_mid + c_in, c_out), bf16),
            pltpu.VMEM(w_reduce2.shape, bf16),
            pltpu.VMEM(w_spatial2.shape, bf16),
            pltpu.VMEM(w_expand2.shape, bf16),
            pltpu.VMEM((batches, ROWS, c_in), bf16),
            pltpu.VMEM((4, ROWS, 128), f32),
            pltpu.VMEM((ROWS, c_in), bf16),
            pltpu.VMEM(bordered, bf16),
            pltpu.VMEM(bordered, bf16),
            pltpu.VMEM(bordered, bf16),
            pltpu.VMEM(bordered, bf16),
            pltpu.VMEM((ROWS, c_mid), bf16),
            pltpu.VMEM((ROWS, c_out), bf16),
            pltpu.VMEM((ROWS, c_out), f32),
            pltpu.VMEM((c_mid, c_out), f32),
            pltpu.VMEM((packed_rows, c_mid), bf16),
            pltpu.VMEM((c_mid, c_mid), bf16),
            pltpu.SemaphoreType.DMA((7,)),
            pltpu.SemaphoreType.DMA((batches,)),
            pltpu.SemaphoreType.DMA((loaders - 1,)),
            pltpu.SemaphoreType.DMA((loaders - 1,)),
        ],
        compiler_params=pltpu.CompilerParams(
            vmem_limit_bytes=60 * 1024 * 1024, collective_id=0, has_side_effects=True
        ),
        name="encode_tiles",
    )(
        slide_counts,
        slide_owner.T,
        b_reduce[None],
        b_spatial[None],
        b_join[None],
        b_reduce2[None],
        b_spatial2[None],
        b_expand2[None],
        tiles,
        w_reduce,
        w_spatial,
        w_expand,
        w_short,
        w_reduce2,
        w_spatial2,
        w_expand2,
    )


def body(tiles, tile_encoder, tile_slot, slide_counts, slide_owner, *weights):
    return encode_local(tiles, slide_counts, slide_owner, *weights)


def solution(mesh):
    split = P(("loader", "enc"))
    placed = (split,) * 5 + (P(),) * 13
    return jax.shard_map(
        body, mesh=mesh, in_specs=placed, out_specs=split, check_vma=False
    )
```

```python
import functools

import jax
import jax.numpy as jnp
from jax import lax
from jax.experimental import pallas as pl
from jax.experimental.pallas import tpu as pltpu
from jax.sharding import PartitionSpec as P

MESH = pl.DeviceIdType.MESH
GRID = 14
CELLS = GRID * GRID
BATCH = 8
ROWS = BATCH * CELLS
LINE = GRID * BATCH
PAIRS = GRID // 2 + 1


def encoder_kernel(
    counts_ref,
    owner_ref,
    b_reduce,
    b_spatial,
    b_join,
    b_reduce2,
    b_spatial2,
    b_expand2,
    tiles,
    w_reduce_hbm,
    w_spatial_hbm,
    w_expand_hbm,
    w_short_hbm,
    w_reduce2_hbm,
    w_spatial2_hbm,
    w_expand2_hbm,
    out,
    w_reduce,
    w_spatial,
    w_join,
    w_reduce2,
    w_spatial2,
    w_expand2,
    arrived,
    widened,
    pixels,
    w_mixed,
    w_mixed2,
    even,
    odd,
    plane,
    sums,
    differences,
    spatial,
    joined,
    residual,
    pooled,
    packed,
    received,
    weight_sem,
    tile_sem,
    send_sem,
    receive_sem,
):
    f32, bf16 = jnp.float32, jnp.bfloat16
    slides = counts_ref.shape[1]
    mid = w_expand_hbm.shape[0]
    most = arrived.shape[0]
    counts = [counts_ref[0, j] for j in range(slides)]
    ends = [counts[0]]
    for count in counts[1:]:
        ends.append(ends[-1] + count)

    loaders = lax.axis_size("loader")
    me = lax.axis_index("loader")
    peers = [lax.rem(me + step, loaders) for step in range(1, loaders)]
    barrier = pltpu.get_barrier_semaphore()
    for peer in peers:
        pl.semaphore_signal(barrier, inc=1, device_id={"loader": peer}, device_id_type=MESH)

    def tile_copy(batch):
        rows = pl.ds(pl.multiple_of(batch * ROWS, ROWS), ROWS)
        return pltpu.make_async_copy(tiles.at[rows], arrived.at[batch], tile_sem.at[batch])

    moves = [
        (w_spatial_hbm, w_spatial),
        (w_spatial2_hbm, w_spatial2),
        (w_reduce_hbm, w_reduce),
        (w_expand_hbm, w_join.at[pl.ds(0, mid)]),
        (w_short_hbm, w_join.at[pl.ds(mid, w_short_hbm.shape[0])]),
        (w_reduce2_hbm, w_reduce2),
        (w_expand2_hbm, w_expand2),
    ]
    copies = [
        pltpu.make_async_copy(source, target, weight_sem.at[index])
        for index, (source, target) in enumerate(moves)
    ]
    tile_copy(0).start()
    for copy in copies:
        copy.start()
    for batch in range(1, most):
        tile_copy(batch).start()

    pooled[...] = jnp.zeros_like(pooled)
    received[packed.shape[0] :, :] = jnp.zeros((mid - packed.shape[0], mid), bf16)

    half = GRID // 2
    pieces = PAIRS - 1
    pair = 2 * BATCH

    def at(i, j):
        return i * pieces + j

    def lanes(n):
        return slice(n * mid, (n + 1) * mid)

    held = {}

    def spread_row(q, m, j, value):
        odd[q, m, j] = value.astype(bf16)
        before = held[q] if j else jnp.zeros((BATCH, mid), f32)
        even[q, m, j] = jnp.concatenate([before, value[:BATCH]], axis=0).astype(bf16)
        held[q] = value[BATCH:]
        if j == pieces - 1:
            after = jnp.zeros((BATCH, mid), f32)
            even[q, m, j + 1] = jnp.concatenate([held[q], after], axis=0).astype(bf16)

    def keep(bias):
        def finish(m, j, n, first, second):
            first = jnp.maximum(first + bias[...], 0.0)
            second = jnp.maximum(second + bias[...], 0.0)
            plane[at(2 * m, j)] = first
            plane[at(2 * m + 1, j)] = second
            spread_row(1, m, j, first + second)
            spread_row(2, m, j, second - first)

        return finish

    def outer(m, nothing):
        for j in range(pieces):
            rows = {
                i: plane[at(i, j) + nothing] for i in range(2 * m - 1, 2 * m + 3) if 0 <= i < GRID
            }
            low = -rows[2 * m + 1]
            if 2 * m - 1 in rows:
                low = rows[2 * m - 1] + low
            high = rows[2 * m]
            if 2 * m + 2 in rows:
                high = high - rows[2 * m + 2]
            spread_row(0, m, j, low)
            spread_row(3, m, j, high)

    combination = ((1, 0), (2, 3))

    def tap(mxu, m, j, n, k):
        q = combination[mxu][n]
        return odd[q, m, j] if k == 1 else even[q, m, j + k // 2]

    def taps(plain, mixed):
        def weights(mxu, n, k):
            q = combination[mxu][n]
            if q in (1, 2):
                return mixed[q - 1, k]
            return plain[lanes((6 if q == 3 else 0) + k)]

        return weights

    def mix(plain, mixed):
        for k in range(3):
            for part in range(4):
                rows = [
                    plain[(3 * a + k) * mid + part * 64 : (3 * a + k) * mid + part * 64 + 64]
                    for a in range(3)
                ]
                rows = [row.astype(f32) * 0.5 for row in rows]
                ends = rows[0] + rows[2]
                mixed[0, k, part * 64 : part * 64 + 64] = (ends + rows[1]).astype(bf16)
                mixed[1, k, part * 64 : part * 64 + 64] = (ends - rows[1]).astype(bf16)

    def convolved(bias, nothing):
        def finish(m, j, n, first, second):
            if n == 0:
                sums[at(m, j)] = first + second
                differences[at(m, j)] = first - second
                return
            first = first + sums[at(m, j) + nothing] + bias[...]
            second = differences[at(m, j) + nothing] - second + bias[...]
            spatial[at(2 * m, j)] = jnp.maximum(first, 0.0).astype(bf16)
            spatial[at(2 * m + 1, j)] = jnp.maximum(second, 0.0).astype(bf16)

        return finish

    def join(m, j, n, *values):
        for i, value in enumerate(values, 2 * m):
            value = jnp.maximum(value + b_join[:, lanes(n)], 0.0)
            joined[at(i, j), :, lanes(n)] = value.astype(bf16)
            residual[at(i, j), :, lanes(n)] = value + b_expand2[:, lanes(n)]

    def tiles_of(ref, nothing):
        return lambda mxu, m, j, n, k: ref[at(2 * m + mxu, j) + nothing, :, lanes(k)]

    def whole(ref):
        return lambda mxu, n, k: ref[lanes(k), lanes(n)]

    def run(stages, *accs):
        passes = []
        for left, weights, width, depth, finish, lag, beside in stages:
            for n in range(width):
                for k in range(depth):
                    ahead = lag if n == 0 else None
                    passes.append((left, weights, finish, n, k, k == depth - 1, ahead, beside))

        def push(index):
            _, weights, _, n, k, _, _, _ = passes[index]
            for mxu in range(2):
                pltpu.matmul_push_rhs(
                    weights(mxu, n, k), staging_register=index % 2, mxu_index=mxu
                )

        def acc(mxu, block, j):
            return accs[(mxu * half + block) * pieces + j]

        def pop(finish, n, block, j):
            finish(block, j, n, *[pltpu.matmul_pop(acc(mxu, block, j)) for mxu in range(2)])

        push(0)
        waiting = None
        for index, (left, weights, finish, n, k, last, lag, beside) in enumerate(passes):
            if index + 1 < len(passes):
                push(index + 1)
            popped = 0
            for block in range(half):
                if waiting is not None and lag is not None:
                    while popped < min(half, block + 1 + lag):
                        for j in range(pieces):
                            pop(*waiting, popped, j)
                        popped += 1
                if beside is not None:
                    beside(n, k, block)
                for j in range(pieces):
                    if waiting is not None and lag is None:
                        pop(*waiting, block, j)
                    for mxu in range(2):
                        pltpu.matmul_acc_lhs(
                            acc(mxu, block, j),
                            left(mxu, block, j, n, k),
                            load_staged_rhs=index % 2 if block + j == 0 else None,
                        )
            waiting = (finish, n) if last else None
        for block in range(half):
            for j in range(pieces):
                pop(*waiting, block, j)

    def widen(batch, i):
        line = slice(i * LINE, (i + 1) * LINE)
        block = arrived[batch, line, :].astype(f32)
        for lane in range(4):
            widened[lane, line, :] = block[:, lane * 128 : (lane + 1) * 128]

    def turn(two_places):
        for lane in range(4):
            two = [
                widened[lane, pl.ds(2 * two_places + k, BATCH, stride=CELLS), :] for k in range(2)
            ]
            pixels[two_places, :, lane * 128 : (lane + 1) * 128] = jnp.concatenate(two, axis=0).astype(bf16)

    tile_copy(0).wait()
    for i in range(GRID):
        widen(0, i)
    for two_places in range(CELLS // 2):
        turn(two_places)

    copies[0].wait()
    mix(w_spatial, w_mixed)
    copies[1].wait()
    mix(w_spatial2, w_mixed2)
    for copy in copies[2:]:
        copy.wait()

    def encode(batch, _):
        pl.when(batch + 1 < most)(lambda: tile_copy(batch + 1).wait())
        following = lax.rem(batch + 1, most)
        totals = {}
        nothing = lax.rem(batch * (batch + 1), 2)

        def first_side(n, k, block):
            if n == 0 and k > 0 and block % 2 == 0 and (k - 1) * 4 + block // 2 < half:
                outer((k - 1) * 4 + block // 2, nothing)
            if n == 1:
                step = k * half + block
                if step < GRID:
                    widen(following, step)

        def second_side(n, k, block):
            if n == 0 and k > 0 and block % 2 == 0 and (k - 1) * 4 + block // 2 < half:
                outer((k - 1) * 4 + block // 2, nothing)
            if n == 1:
                step = k * half + block
                for two_places in range(5 * step, 5 * step + 5):
                    if two_places < CELLS // 2:
                        turn(two_places)

        def pool(m, j, n, *values):
            for i, value in enumerate(values, 2 * m):
                value = jnp.maximum(value + residual[at(i, j) + nothing, :, lanes(n)], 0.0)
                value = value[:BATCH] + value[BATCH:]
                totals[n] = totals[n] + value if n in totals else value

        def both(mxu, m, j, n, k):
            if k == 0:
                return spatial[at(2 * m + mxu, j) + nothing]
            return pixels[at(2 * m + mxu, j), :, lanes(k - 1)]

        wide = joined.shape[2] // mid
        deep = pixels.shape[2] // mid
        stages = [
            (tiles_of(pixels, 0), whole(w_reduce), 1, deep, keep(b_reduce), 0, None),
            (tap, taps(w_spatial, w_mixed), 2, 3, convolved(b_spatial, nothing), 1, first_side),
            (both, whole(w_join), wide, deep + 1, join, 1, None),
            (tiles_of(joined, nothing), whole(w_reduce2), 1, wide, keep(b_reduce2), 1, None),
            (tap, taps(w_spatial2, w_mixed2), 2, 3, convolved(b_spatial2, nothing), 1, second_side),
            (tiles_of(spatial, nothing), whole(w_expand2), wide, 1, pool, 1, None),
        ]
        accumulators = [
            pltpu.ACC(mxu)((pair, mid), f32)
            for mxu in range(2)
            for _ in range(half * pieces)
        ]

        def all_stages(*accs):
            run(stages, *accs)
            rows = pl.ds(pl.multiple_of(batch * BATCH, BATCH), BATCH)
            for n, total in totals.items():
                pooled[rows, lanes(n)] = total / CELLS

        pl.run_scoped(all_stages, *accumulators)
        return 0

    lax.fori_loop(0, most, encode, 0)

    rows = packed.shape[0]
    width = pooled.shape[1] // mid
    cap = rows // (loaders * width)
    row = lax.broadcasted_iota(jnp.int32, (rows, mid), 0)
    place = lax.broadcasted_iota(jnp.int32, (rows, mid), 1)
    column = lax.broadcasted_iota(jnp.int32, (rows, 1), 0)
    divisor = jnp.ones((rows, 1), f32)
    owners = [owner_ref[0, j] for j in range(slides)]
    chosen = jnp.zeros((rows, mid), f32)
    slot = row // (width * cap) * cap + row % cap
    slot_column = column // (width * cap) * cap + column % cap
    for j in range(slides):
        standing = jnp.int32(0)
        for earlier in range(j):
            standing += (owners[earlier] == owners[j]).astype(jnp.int32)
        target = owners[j] * cap + standing
        member = (slot == target) & (place >= ends[j] - counts[j]) & (place < ends[j])
        chosen = jnp.where(member, 1.0, chosen)
        size = jnp.maximum(counts[j], 1).astype(f32)
        divisor = jnp.where(slot_column == target, size, divisor)

    def average(acc):
        for n in range(width):
            pltpu.matmul_push_rhs(
                pooled[:, lanes(n)].astype(bf16), staging_register=n % 2, mxu_index=0
            )
            here = jnp.where(row // cap % width == n, chosen, 0.0).astype(bf16)
            pltpu.matmul_acc_lhs(acc, here, load_staged_rhs=n % 2)
        packed[...] = (pltpu.matmul_pop(acc) / divisor).astype(bf16)

    pl.run_scoped(average, pltpu.ACC(0)((rows, mid), f32))

    size = width * cap

    def block(index):
        return pl.ds(pl.multiple_of(index * size, size), size)

    pl.semaphore_wait(barrier, loaders - 1)
    sends = [
        pltpu.make_async_remote_copy(
            src_ref=packed.at[block(peer)],
            dst_ref=received.at[block(me)],
            send_sem=send_sem.at[index],
            recv_sem=receive_sem.at[index],
            device_id={"loader": peer},
            device_id_type=MESH,
        )
        for index, peer in enumerate(peers)
    ]
    for send in sends:
        send.start()
    received[block(me), :] = packed[block(me), :]

    shape = (out.shape[0], mid)
    row = lax.broadcasted_iota(jnp.int32, shape, 0)
    column = lax.broadcasted_iota(jnp.int32, shape, 1)

    def unpack(*accs):
        pltpu.matmul_push_rhs(received[...], staging_register=0, mxu_index=0)
        for n, acc in enumerate(accs):
            source = (row // cap * width + n) * cap + row % cap
            here = jnp.where(column == source, 1.0, 0.0).astype(bf16)
            pltpu.matmul_acc_lhs(acc, here, load_staged_rhs=0 if n == 0 else None)
        for n, acc in enumerate(accs):
            out[:, lanes(n)] = pltpu.matmul_pop(acc).astype(bf16)

    for send in sends:
        send.wait()
    pl.run_scoped(unpack, *[pltpu.ACC(0)(shape, f32) for _ in range(width)])


def encode_local(
    tiles,
    slide_counts,
    slide_owner,
    w_reduce,
    b_reduce,
    w_spatial,
    b_spatial,
    w_expand,
    w_short,
    b_join,
    w_reduce2,
    b_reduce2,
    w_spatial2,
    b_spatial2,
    w_expand2,
    b_expand2,
):
    bf16, f32 = jnp.bfloat16, jnp.float32
    places = tiles.shape[0] // CELLS
    c_in, c_mid = w_reduce.shape
    c_out = w_expand.shape[1]
    loaders = lax.axis_size("loader")
    packed_rows = places * (c_out // c_mid)
    batches = places // BATCH
    smem = pl.BlockSpec(memory_space=pltpu.SMEM)
    vmem = pl.BlockSpec(memory_space=pltpu.VMEM)
    anywhere = pl.BlockSpec(memory_space=pl.ANY)
    return pl.pallas_call(
        encoder_kernel,
        out_shape=jax.ShapeDtypeStruct((places, c_out), bf16),
        in_specs=[smem] * 2 + [vmem] * 6 + [anywhere] * 8,
        out_specs=vmem,
        scratch_shapes=[
            pltpu.VMEM(w_reduce.shape, bf16),
            pltpu.VMEM(w_spatial.shape, bf16),
            pltpu.VMEM((c_mid + c_in, c_out), bf16),
            pltpu.VMEM(w_reduce2.shape, bf16),
            pltpu.VMEM(w_spatial2.shape, bf16),
            pltpu.VMEM(w_expand2.shape, bf16),
            pltpu.VMEM((batches, ROWS, c_in), bf16),
            pltpu.VMEM((4, ROWS, 128), f32),
            pltpu.VMEM((CELLS // 2, 2 * BATCH, c_in), bf16),
            pltpu.VMEM((2, 3, c_mid, c_mid), bf16),
            pltpu.VMEM((2, 3, c_mid, c_mid), bf16),
            pltpu.VMEM((4, GRID // 2, PAIRS, 2 * BATCH, c_mid), bf16),
            pltpu.VMEM((4, GRID // 2, PAIRS - 1, 2 * BATCH, c_mid), bf16),
            pltpu.VMEM((CELLS // 2, 2 * BATCH, c_mid), f32),
            pltpu.VMEM((CELLS // 4, 2 * BATCH, c_mid), f32),
            pltpu.VMEM((CELLS // 4, 2 * BATCH, c_mid), f32),
            pltpu.VMEM((CELLS // 2, 2 * BATCH, c_mid), bf16),
            pltpu.VMEM((CELLS // 2, 2 * BATCH, c_out), bf16),
            pltpu.VMEM((CELLS // 2, 2 * BATCH, c_out), f32),
            pltpu.VMEM((c_mid, c_out), f32),
            pltpu.VMEM((packed_rows, c_mid), bf16),
            pltpu.VMEM((c_mid, c_mid), bf16),
            pltpu.SemaphoreType.DMA((7,)),
            pltpu.SemaphoreType.DMA((batches,)),
            pltpu.SemaphoreType.DMA((loaders - 1,)),
            pltpu.SemaphoreType.DMA((loaders - 1,)),
        ],
        compiler_params=pltpu.CompilerParams(
            vmem_limit_bytes=60 * 1024 * 1024, collective_id=0, has_side_effects=True
        ),
        name="encode_tiles",
    )(
        slide_counts,
        slide_owner.T,
        b_reduce[None],
        b_spatial[None],
        b_join[None],
        b_reduce2[None],
        b_spatial2[None],
        b_expand2[None],
        tiles,
        w_reduce,
        w_spatial,
        w_expand,
        w_short,
        w_reduce2,
        w_spatial2,
        w_expand2,
    )


def body(tiles, tile_encoder, tile_slot, slide_counts, slide_owner, *weights):
    return encode_local(tiles, slide_counts, slide_owner, *weights)


def solution(mesh):
    split = P(("loader", "enc"))
    placed = (split,) * 5 + (P(),) * 13
    return jax.shard_map(
        body, mesh=mesh, in_specs=placed, out_specs=split, check_vma=False
    )
```

```python
import functools

import jax
import jax.numpy as jnp
from jax import lax
from jax.experimental import pallas as pl
from jax.experimental.pallas import tpu as pltpu
from jax.sharding import PartitionSpec as P

MESH = pl.DeviceIdType.MESH
GRID = 14
CELLS = GRID * GRID
BATCH = 8
ROWS = BATCH * CELLS
LINE = GRID * BATCH
PAIRS = GRID // 2 + 1


def encoder_kernel(
    counts_ref,
    owner_ref,
    b_reduce,
    b_spatial,
    b_join,
    b_reduce2,
    b_spatial2,
    b_expand2,
    tiles,
    w_reduce_hbm,
    w_spatial_hbm,
    w_expand_hbm,
    w_short_hbm,
    w_reduce2_hbm,
    w_spatial2_hbm,
    w_expand2_hbm,
    out,
    w_reduce,
    w_spatial,
    w_join,
    w_reduce2,
    w_spatial2,
    w_expand2,
    arrived,
    widened,
    pixels,
    w_mixed,
    w_mixed2,
    even,
    odd,
    plane,
    sums,
    differences,
    spatial,
    joined,
    residual,
    pooled,
    packed,
    received,
    weight_sem,
    tile_sem,
    send_sem,
    receive_sem,
):
    f32, bf16 = jnp.float32, jnp.bfloat16
    slides = counts_ref.shape[1]
    mid = w_expand_hbm.shape[0]
    most = arrived.shape[0]
    counts = [counts_ref[0, j] for j in range(slides)]
    ends = [counts[0]]
    for count in counts[1:]:
        ends.append(ends[-1] + count)

    loaders = lax.axis_size("loader")
    me = lax.axis_index("loader")
    peers = [lax.rem(me + step, loaders) for step in range(1, loaders)]
    barrier = pltpu.get_barrier_semaphore()
    for peer in peers:
        pl.semaphore_signal(barrier, inc=1, device_id={"loader": peer}, device_id_type=MESH)

    def tile_copy(batch):
        rows = pl.ds(pl.multiple_of(batch * ROWS, ROWS), ROWS)
        return pltpu.make_async_copy(tiles.at[rows], arrived.at[batch], tile_sem.at[batch])

    moves = [
        (w_spatial_hbm, w_spatial),
        (w_spatial2_hbm, w_spatial2),
        (w_reduce_hbm, w_reduce),
        (w_expand_hbm, w_join.at[pl.ds(0, mid)]),
        (w_short_hbm, w_join.at[pl.ds(mid, w_short_hbm.shape[0])]),
        (w_reduce2_hbm, w_reduce2),
        (w_expand2_hbm, w_expand2),
    ]
    copies = [
        pltpu.make_async_copy(source, target, weight_sem.at[index])
        for index, (source, target) in enumerate(moves)
    ]
    tile_copy(0).start()
    for copy in copies:
        copy.start()
    for batch in range(1, most):
        tile_copy(batch).start()

    pooled[...] = jnp.zeros_like(pooled)
    received[packed.shape[0] :, :] = jnp.zeros((mid - packed.shape[0], mid), bf16)

    half = GRID // 2
    pieces = PAIRS - 1
    pair = 2 * BATCH

    def at(i, j):
        return i * pieces + j

    def lanes(n):
        return slice(n * mid, (n + 1) * mid)

    held = {}

    def spread_row(q, m, j, value):
        odd[q, m, j] = value.astype(bf16)
        before = held[q] if j else jnp.zeros((BATCH, mid), f32)
        even[q, m, j] = jnp.concatenate([before, value[:BATCH]], axis=0).astype(bf16)
        held[q] = value[BATCH:]
        if j == pieces - 1:
            after = jnp.zeros((BATCH, mid), f32)
            even[q, m, j + 1] = jnp.concatenate([held[q], after], axis=0).astype(bf16)

    def keep(bias):
        def finish(m, j, n, first, second):
            first = jnp.maximum(first + bias[...], 0.0)
            second = jnp.maximum(second + bias[...], 0.0)
            plane[at(2 * m, j)] = first
            plane[at(2 * m + 1, j)] = second
            spread_row(1, m, j, first + second)
            spread_row(2, m, j, second - first)

        return finish

    def outer(m, nothing):
        for j in range(pieces):
            rows = {
                i: plane[at(i, j) + nothing] for i in range(2 * m - 1, 2 * m + 3) if 0 <= i < GRID
            }
            low = -rows[2 * m + 1]
            if 2 * m - 1 in rows:
                low = rows[2 * m - 1] + low
            high = rows[2 * m]
            if 2 * m + 2 in rows:
                high = high - rows[2 * m + 2]
            spread_row(0, m, j, low)
            spread_row(3, m, j, high)

    combination = ((1, 0), (2, 3))

    def tap(mxu, m, j, n, k):
        q = combination[mxu][n]
        return odd[q, m, j] if k == 1 else even[q, m, j + k // 2]

    def taps(plain, mixed):
        def weights(mxu, n, k):
            q = combination[mxu][n]
            if q in (1, 2):
                return mixed[q - 1, k]
            return plain[lanes((6 if q == 3 else 0) + k)]

        return weights

    def mix(plain, mixed):
        for k in range(3):
            for part in range(4):
                rows = [
                    plain[(3 * a + k) * mid + part * 64 : (3 * a + k) * mid + part * 64 + 64]
                    for a in range(3)
                ]
                rows = [row.astype(f32) * 0.5 for row in rows]
                ends = rows[0] + rows[2]
                mixed[0, k, part * 64 : part * 64 + 64] = (ends + rows[1]).astype(bf16)
                mixed[1, k, part * 64 : part * 64 + 64] = (ends - rows[1]).astype(bf16)

    def convolved(bias, nothing):
        def finish(m, j, n, first, second):
            if n == 0:
                sums[at(m, j)] = first + second
                differences[at(m, j)] = first - second
                return
            first = first + sums[at(m, j) + nothing] + bias[...]
            second = differences[at(m, j) + nothing] - second + bias[...]
            spatial[at(2 * m, j)] = jnp.maximum(first, 0.0).astype(bf16)
            spatial[at(2 * m + 1, j)] = jnp.maximum(second, 0.0).astype(bf16)

        return finish

    def join(m, j, n, *values):
        for i, value in enumerate(values, 2 * m):
            value = jnp.maximum(value + b_join[:, lanes(n)], 0.0)
            joined[at(i, j), :, lanes(n)] = value.astype(bf16)
            residual[at(i, j), :, lanes(n)] = value + b_expand2[:, lanes(n)]

    def tiles_of(ref, nothing):
        return lambda mxu, m, j, n, k: ref[at(2 * m + mxu, j) + nothing, :, lanes(k)]

    def whole(ref):
        return lambda mxu, n, k: ref[lanes(k), lanes(n)]

    def run(stages, *accs):
        passes = []
        for left, weights, width, depth, finish, lag, beside in stages:
            for n in range(width):
                for k in range(depth):
                    ahead = lag if n == 0 else None
                    passes.append((left, weights, finish, n, k, k == depth - 1, ahead, beside))

        def push(index):
            _, weights, _, n, k, _, _, _ = passes[index]
            for mxu in range(2):
                pltpu.matmul_push_rhs(
                    weights(mxu, n, k), staging_register=index % 2, mxu_index=mxu
                )

        def acc(mxu, block, j):
            return accs[(mxu * half + block) * pieces + j]

        def pop(finish, n, block, j):
            finish(block, j, n, *[pltpu.matmul_pop(acc(mxu, block, j)) for mxu in range(2)])

        push(0)
        waiting = None
        for index, (left, weights, finish, n, k, last, lag, beside) in enumerate(passes):
            if index + 1 < len(passes):
                push(index + 1)
            popped = 0
            for block in range(half):
                if waiting is not None and lag is not None:
                    while popped < min(half, block + 1 + lag):
                        for j in range(pieces):
                            pop(*waiting, popped, j)
                        popped += 1
                if beside is not None:
                    beside(n, k, block)
                for j in range(pieces):
                    if waiting is not None and lag is None:
                        pop(*waiting, block, j)
                    for mxu in range(2):
                        pltpu.matmul_acc_lhs(
                            acc(mxu, block, j),
                            left(mxu, block, j, n, k),
                            load_staged_rhs=index % 2 if block + j == 0 else None,
                        )
            waiting = (finish, n) if last else None
        for block in range(half):
            for j in range(pieces):
                pop(*waiting, block, j)

    def widen(batch, i):
        line = slice(i * LINE, (i + 1) * LINE)
        block = arrived[batch, line, :].astype(f32)
        for lane in range(4):
            widened[lane, line, :] = block[:, lane * 128 : (lane + 1) * 128]

    def turn(two_places):
        for lane in range(4):
            two = [
                widened[lane, pl.ds(2 * two_places + k, BATCH, stride=CELLS), :] for k in range(2)
            ]
            pixels[two_places, :, lane * 128 : (lane + 1) * 128] = jnp.concatenate(two, axis=0).astype(bf16)

    tile_copy(0).wait()
    for i in range(GRID):
        widen(0, i)
    for two_places in range(CELLS // 2):
        turn(two_places)

    copies[0].wait()
    mix(w_spatial, w_mixed)
    copies[1].wait()
    mix(w_spatial2, w_mixed2)
    for copy in copies[2:]:
        copy.wait()

    def encode(batch, _):
        @pl.when(batch + 1 < most)
        def _():
            tile_copy(batch + 1).wait()
            for i in range(GRID):
                widen(batch + 1, i)

        totals = {}
        nothing = lax.rem(batch * (batch + 1), 2)

        def first_side(n, k, block):
            if n == 0 and k > 0 and block % 2 == 0 and (k - 1) * 4 + block // 2 < half:
                outer((k - 1) * 4 + block // 2, nothing)

        def second_side(n, k, block):
            if n == 0 and k > 0 and block % 2 == 0 and (k - 1) * 4 + block // 2 < half:
                outer((k - 1) * 4 + block // 2, nothing)
            if n == 1:
                step = k * half + block
                for two_places in range(5 * step, 5 * step + 5):
                    if two_places < CELLS // 2:
                        turn(two_places)

        def pool(m, j, n, *values):
            for i, value in enumerate(values, 2 * m):
                value = jnp.maximum(value + residual[at(i, j) + nothing, :, lanes(n)], 0.0)
                value = value[:BATCH] + value[BATCH:]
                totals[n] = totals[n] + value if n in totals else value

        def both(mxu, m, j, n, k):
            if k == 0:
                return spatial[at(2 * m + mxu, j) + nothing]
            return pixels[at(2 * m + mxu, j), :, lanes(k - 1)]

        wide = joined.shape[2] // mid
        deep = pixels.shape[2] // mid
        stages = [
            (tiles_of(pixels, 0), whole(w_reduce), 1, deep, keep(b_reduce), 0, None),
            (tap, taps(w_spatial, w_mixed), 2, 3, convolved(b_spatial, nothing), 1, first_side),
            (both, whole(w_join), wide, deep + 1, join, 1, None),
            (tiles_of(joined, nothing), whole(w_reduce2), 1, wide, keep(b_reduce2), 1, None),
            (tap, taps(w_spatial2, w_mixed2), 2, 3, convolved(b_spatial2, nothing), 1, second_side),
            (tiles_of(spatial, nothing), whole(w_expand2), wide, 1, pool, 1, None),
        ]
        accumulators = [
            pltpu.ACC(mxu)((pair, mid), f32)
            for mxu in range(2)
            for _ in range(half * pieces)
        ]

        def all_stages(*accs):
            run(stages, *accs)
            rows = pl.ds(pl.multiple_of(batch * BATCH, BATCH), BATCH)
            for n, total in totals.items():
                pooled[rows, lanes(n)] = total / CELLS

        pl.run_scoped(all_stages, *accumulators)
        return 0

    lax.fori_loop(0, most, encode, 0)

    rows = packed.shape[0]
    width = pooled.shape[1] // mid
    cap = rows // (loaders * width)
    row = lax.broadcasted_iota(jnp.int32, (rows, mid), 0)
    place = lax.broadcasted_iota(jnp.int32, (rows, mid), 1)
    column = lax.broadcasted_iota(jnp.int32, (rows, 1), 0)
    divisor = jnp.ones((rows, 1), f32)
    owners = [owner_ref[0, j] for j in range(slides)]
    chosen = jnp.zeros((rows, mid), f32)
    slot = row // (width * cap) * cap + row % cap
    slot_column = column // (width * cap) * cap + column % cap
    for j in range(slides):
        standing = jnp.int32(0)
        for earlier in range(j):
            standing += (owners[earlier] == owners[j]).astype(jnp.int32)
        target = owners[j] * cap + standing
        member = (slot == target) & (place >= ends[j] - counts[j]) & (place < ends[j])
        chosen = jnp.where(member, 1.0, chosen)
        size = jnp.maximum(counts[j], 1).astype(f32)
        divisor = jnp.where(slot_column == target, size, divisor)

    def average(acc):
        for n in range(width):
            pltpu.matmul_push_rhs(
                pooled[:, lanes(n)].astype(bf16), staging_register=n % 2, mxu_index=0
            )
            here = jnp.where(row // cap % width == n, chosen, 0.0).astype(bf16)
            pltpu.matmul_acc_lhs(acc, here, load_staged_rhs=n % 2)
        packed[...] = (pltpu.matmul_pop(acc) / divisor).astype(bf16)

    pl.run_scoped(average, pltpu.ACC(0)((rows, mid), f32))

    size = width * cap

    def block(index):
        return pl.ds(pl.multiple_of(index * size, size), size)

    pl.semaphore_wait(barrier, loaders - 1)
    sends = [
        pltpu.make_async_remote_copy(
            src_ref=packed.at[block(peer)],
            dst_ref=received.at[block(me)],
            send_sem=send_sem.at[index],
            recv_sem=receive_sem.at[index],
            device_id={"loader": peer},
            device_id_type=MESH,
        )
        for index, peer in enumerate(peers)
    ]
    for send in sends:
        send.start()
    received[block(me), :] = packed[block(me), :]

    shape = (out.shape[0], mid)
    row = lax.broadcasted_iota(jnp.int32, shape, 0)
    column = lax.broadcasted_iota(jnp.int32, shape, 1)

    def unpack(*accs):
        pltpu.matmul_push_rhs(received[...], staging_register=0, mxu_index=0)
        for n, acc in enumerate(accs):
            source = (row // cap * width + n) * cap + row % cap
            here = jnp.where(column == source, 1.0, 0.0).astype(bf16)
            pltpu.matmul_acc_lhs(acc, here, load_staged_rhs=0 if n == 0 else None)
        for n, acc in enumerate(accs):
            out[:, lanes(n)] = pltpu.matmul_pop(acc).astype(bf16)

    for send in sends:
        send.wait()
    pl.run_scoped(unpack, *[pltpu.ACC(0)(shape, f32) for _ in range(width)])


def encode_local(
    tiles,
    slide_counts,
    slide_owner,
    w_reduce,
    b_reduce,
    w_spatial,
    b_spatial,
    w_expand,
    w_short,
    b_join,
    w_reduce2,
    b_reduce2,
    w_spatial2,
    b_spatial2,
    w_expand2,
    b_expand2,
):
    bf16, f32 = jnp.bfloat16, jnp.float32
    places = tiles.shape[0] // CELLS
    c_in, c_mid = w_reduce.shape
    c_out = w_expand.shape[1]
    loaders = lax.axis_size("loader")
    packed_rows = places * (c_out // c_mid)
    batches = places // BATCH
    smem = pl.BlockSpec(memory_space=pltpu.SMEM)
    vmem = pl.BlockSpec(memory_space=pltpu.VMEM)
    anywhere = pl.BlockSpec(memory_space=pl.ANY)
    return pl.pallas_call(
        encoder_kernel,
        out_shape=jax.ShapeDtypeStruct((places, c_out), bf16),
        in_specs=[smem] * 2 + [vmem] * 6 + [anywhere] * 8,
        out_specs=vmem,
        scratch_shapes=[
            pltpu.VMEM(w_reduce.shape, bf16),
            pltpu.VMEM(w_spatial.shape, bf16),
            pltpu.VMEM((c_mid + c_in, c_out), bf16),
            pltpu.VMEM(w_reduce2.shape, bf16),
            pltpu.VMEM(w_spatial2.shape, bf16),
            pltpu.VMEM(w_expand2.shape, bf16),
            pltpu.VMEM((batches, ROWS, c_in), bf16),
            pltpu.VMEM((4, ROWS, 128), f32),
            pltpu.VMEM((CELLS // 2, 2 * BATCH, c_in), bf16),
            pltpu.VMEM((2, 3, c_mid, c_mid), bf16),
            pltpu.VMEM((2, 3, c_mid, c_mid), bf16),
            pltpu.VMEM((4, GRID // 2, PAIRS, 2 * BATCH, c_mid), bf16),
            pltpu.VMEM((4, GRID // 2, PAIRS - 1, 2 * BATCH, c_mid), bf16),
            pltpu.VMEM((CELLS // 2, 2 * BATCH, c_mid), f32),
            pltpu.VMEM((CELLS // 4, 2 * BATCH, c_mid), f32),
            pltpu.VMEM((CELLS // 4, 2 * BATCH, c_mid), f32),
            pltpu.VMEM((CELLS // 2, 2 * BATCH, c_mid), bf16),
            pltpu.VMEM((CELLS // 2, 2 * BATCH, c_out), bf16),
            pltpu.VMEM((CELLS // 2, 2 * BATCH, c_out), f32),
            pltpu.VMEM((c_mid, c_out), f32),
            pltpu.VMEM((packed_rows, c_mid), bf16),
            pltpu.VMEM((c_mid, c_mid), bf16),
            pltpu.SemaphoreType.DMA((7,)),
            pltpu.SemaphoreType.DMA((batches,)),
            pltpu.SemaphoreType.DMA((loaders - 1,)),
            pltpu.SemaphoreType.DMA((loaders - 1,)),
        ],
        compiler_params=pltpu.CompilerParams(
            vmem_limit_bytes=60 * 1024 * 1024, collective_id=0, has_side_effects=True
        ),
        name="encode_tiles",
    )(
        slide_counts,
        slide_owner.T,
        b_reduce[None],
        b_spatial[None],
        b_join[None],
        b_reduce2[None],
        b_spatial2[None],
        b_expand2[None],
        tiles,
        w_reduce,
        w_spatial,
        w_expand,
        w_short,
        w_reduce2,
        w_spatial2,
        w_expand2,
    )


def body(tiles, tile_encoder, tile_slot, slide_counts, slide_owner, *weights):
    return encode_local(tiles, slide_counts, slide_owner, *weights)


def solution(mesh):
    split = P(("loader", "enc"))
    placed = (split,) * 5 + (P(),) * 13
    return jax.shard_map(
        body, mesh=mesh, in_specs=placed, out_specs=split, check_vma=False
    )
```
